128 devices in a mesh: row: 32 (over x, y, core), col: 4 (over z).
Axes of the slice: x: 4, y: 4, z: 4, core: 2. Of those that a mesh axis runs over, the one named last changes fastest.
Arguments:
- tokens: bfloat16 [8192, 1024], P('row', 'col'), may hold values from -6 to 6
- run_counts: int32 [32], replicated, may hold values from 128 to 256, as said below
- seq_lengths: int32 [8], replicated, may hold values from 1 to 8192, as said below
- first_gain: bfloat16 [1024], P('col'), may hold values from 0.099609375 to 1.8984375
- in_weight: bfloat16 [1024, 3, 1024], P('row', None, 'col'), may hold values from -0.1875 to 0.1875
- conv_weight: bfloat16 [3, 1024], P(None, 'col'), may hold values from -3 to 3
- out_weight: bfloat16 [1024, 1024], P('row', 'col'), may hold values from -0.1875 to 0.1875
- second_gain: bfloat16 [1024], P('col'), may hold values from 0.099609375 to 1.8984375
- gate_weight: bfloat16 [1024, 4608], P('row', 'col'), may hold values from -0.1875 to 0.1875
- up_weight: bfloat16 [1024, 4608], P('row', 'col'), may hold values from -0.1875 to 0.1875
- down_weight: bfloat16 [4608, 1024], P('row', 'col'), may hold values from -0.125 to 0.125
- cotangent: bfloat16 [8192, 1024], P('row', 'col'), may hold values from -6 to 6
Outputs:
- block_out: bfloat16 [8192, 1024], P('row', 'col')
- input_grad: float32 [8192, 1024], P('row', 'col')
- first_gain_grad: float32 [1024], P('col')
- in_weight_grad: float32 [1024, 3, 1024], P('row', None, 'col')
- conv_weight_grad: float32 [3, 1024], P(None, 'col')
- out_weight_grad: float32 [1024, 1024], P('row', 'col')
- second_gain_grad: float32 [1024], P('col')
- gate_grad: float32 [1024, 4608], P('row', 'col')
- up_grad: float32 [1024, 4608], P('row', 'col')
- down_grad: float32 [4608, 1024], P('row', 'col')
The draws below stay inside these ranges and needn't reach their ends.
Inputs may be any that keep to these rules, and one draw needn't show every extreme that they name: `run_counts`: some index of row holds exactly 256 live tokens and another exactly 128. `seq_lengths`: exactly one sequence, at an index that varies, is 8192 long; the sequences before it are together shorter than 128.
All inputs are finite; a program needn't handle non-finite values.
Results may differ from the reference program's by a relative error of at most 0.015.
Values may be sent and summed in bfloat16 or wider, within the bound.
A program may use at most 64 MiB of HBM per device.

```python
import jax
import jax.numpy as jnp
from jax import lax

D = 1024
FF = 4608
CAP = 256
SLOTS = 8192
SEQ_MAX = 8192
NSEQ = 8
N_ROW = 32


def draw_run_counts(key, part):
    key = jax.random.fold_in(key, 11)
    key_base, key_full, key_half = jax.random.split(key, 3)
    base = jax.random.randint(key_base, (N_ROW,), CAP // 2, CAP + 1)
    full_at = jax.random.randint(key_full, (), 0, N_ROW)
    half_at = (full_at + 1 + jax.random.randint(key_half, (), 0, N_ROW - 1)) % N_ROW
    run_ids = jnp.arange(N_ROW)
    counts = jnp.where(run_ids == full_at, CAP, base)
    counts = jnp.where(run_ids == half_at, CAP // 2, counts)
    return counts.astype(jnp.int32)


def draw_seq_lengths(key, part):
    key = jax.random.fold_in(key, 12)
    key_pick, key_head, key_tail = jax.random.split(key, 3)
    long_at = jax.random.randint(key_pick, (), 0, NSEQ)
    head_most = max(1, CAP // 2 // NSEQ)
    head = jax.random.randint(key_head, (NSEQ,), 1, head_most + 1)
    tail = jax.random.randint(key_tail, (NSEQ,), 1, CAP + 1)
    seq_ids = jnp.arange(NSEQ)
    lengths = jnp.where(seq_ids < long_at, head, jnp.where(seq_ids == long_at, SEQ_MAX, tail))
    return lengths.astype(jnp.int32)


def levels(rng, extent, cuts, least, largest):
    def one(dim, shards_of):
        steps = jax.random.uniform(jax.random.fold_in(jax.random.fold_in(rng, 6), dim), (shards_of,), jnp.float32, least / len(cuts), largest / len(cuts))
        return jnp.repeat(jnp.exp(steps), extent[dim] // shards_of).reshape((-1,) + (1,) * (len(extent) - dim - 1))

    loudness = one(*cuts[0])
    for cut in cuts[1:]:
        loudness = loudness * one(*cut)
    return loudness


def normal_values(rng, extent, width, bound, cuts=(), held_as=jnp.bfloat16):
    array = width * jax.random.normal(rng, extent, jnp.float32)
    if cuts:
        array = array * levels(rng, extent, cuts, -0.22, 0.18)
    return jnp.clip(array, -bound, bound).astype(held_as)


def setup_inputs(seed: int = 0) -> dict:
    keys = jax.random.split(jax.random.key(seed), 13)
    tokens = normal_values(keys[0], (SLOTS, D), 1.0, 6.0, ((0, 32), (1, 4)))
    run_counts = draw_run_counts(jax.random.fold_in(keys[12], 71), 0)
    seq_lengths = draw_seq_lengths(jax.random.fold_in(keys[12], 71), 0)
    first_gain = jnp.clip(1.0 + 0.18 * jax.random.normal(keys[3], (D,), jnp.float32), 0.099609375, 1.8984375).astype(jnp.bfloat16)
    in_weight = normal_values(keys[4], (D, 3, D), D ** -0.5, 0.1875, ((0, 32), (2, 4)))
    conv_weight = normal_values(keys[5], (3, D), 0.6, 3.0, ((1, 4),))
    out_weight = normal_values(keys[6], (D, D), D ** -0.5, 0.1875, ((0, 32), (1, 4)))
    second_gain = jnp.clip(1.0 + 0.18 * jax.random.normal(keys[7], (D,), jnp.float32), 0.099609375, 1.8984375).astype(jnp.bfloat16)
    gate_weight = normal_values(keys[8], (D, FF), D ** -0.5, 0.1875, ((0, 32), (1, 4)))
    up_weight = normal_values(keys[9], (D, FF), D ** -0.5, 0.1875, ((0, 32), (1, 4)))
    down_weight = normal_values(keys[10], (FF, D), (FF // 2) ** -0.5, 0.125, ((0, 32), (1, 4)))
    cotangent = normal_values(keys[11], (SLOTS, D), 1.0, 6.0, ((0, 32), (1, 4)))
    return dict(tokens=tokens, run_counts=run_counts, seq_lengths=seq_lengths, first_gain=first_gain, in_weight=in_weight, conv_weight=conv_weight, out_weight=out_weight, second_gain=second_gain, gate_weight=gate_weight, up_weight=up_weight, down_weight=down_weight, cotangent=cotangent)


@jax.custom_vjp
def low(v):
    return lax.optimization_barrier(v.astype(jnp.bfloat16)).astype(jnp.float32)

@jax.custom_vjp
def low_back(v):
    return v

def low_keep(v):
    return (low(v), None)

def low_pass(kept, grad):
    return (grad,)

def back_keep(v):
    return (v, None)

def back_low(kept, grad):
    return (low(grad),)
low.defvjp(low_keep, low_pass)
low_back.defvjp(back_keep, back_low)
epsilon = 1e-05
highest = lax.Precision.HIGHEST

def rms_scale(values):
    return values * lax.rsqrt(lax.optimization_barrier(jnp.mean(values * values, axis=-1, keepdims=True)) + epsilon)

def slot_tables(run_counts, seq_lengths):
    slot_ids = jnp.arange(SLOTS, dtype=jnp.int32)
    run_ids = slot_ids // CAP
    within = slot_ids % CAP
    offsets = (jnp.cumsum(run_counts) - run_counts).astype(jnp.int32)
    own_count = jnp.take(run_counts, run_ids)
    position = jnp.take(offsets, run_ids) + within
    live = within < own_count
    starts = (jnp.cumsum(seq_lengths) - seq_lengths).astype(jnp.int32)
    seq_start = lax.optimization_barrier(jnp.max(jnp.where(starts[None, :] <= position[:, None], starts[None, :], 0), axis=1))
    prev_count = jnp.take(run_counts, jnp.maximum(run_ids - 1, 0))
    sources = []
    valids = []
    for shift_by in (1, 2):
        local_src = slot_ids - shift_by
        remote_src = (run_ids - 1) * CAP + prev_count - (shift_by - within)
        source = jnp.clip(jnp.where(within >= shift_by, local_src, remote_src), 0, SLOTS - 1).astype(jnp.int32)
        valid = live & (position - shift_by >= seq_start)
        sources.append(source)
        valids.append(valid.astype(jnp.float32)[:, None])
    return (live.astype(jnp.float32)[:, None], sources, valids)

def forward_block(tables, x_in, gain_one, w_in, w_conv, w_out, gain_two, w_gate, w_up, w_down):
    live, sources, valids = tables
    h_one = low(rms_scale(x_in) * gain_one)
    proj = low_back(jnp.einsum('sd,dpe->spe', h_one, w_in, precision=highest))
    b_part = proj[:, 0]
    c_part = proj[:, 1]
    x_part = proj[:, 2]
    prod = low(b_part * x_part)
    conv = w_conv[0] * prod
    conv = conv + w_conv[1] * valids[0] * jnp.take(prod, sources[0], axis=0)
    conv = conv + w_conv[2] * valids[1] * jnp.take(prod, sources[1], axis=0)
    mixed = low(c_part * conv)
    branch = low_back(jnp.dot(mixed, w_out, precision=highest))
    resid = x_in + branch
    h_two = low(rms_scale(resid) * gain_two)
    gate = low_back(jnp.dot(h_two, w_gate, precision=highest))
    upval = low_back(jnp.dot(h_two, w_up, precision=highest))
    hidden = low(jax.nn.silu(gate) * upval)
    ffn_out = low_back(jnp.dot(hidden, w_down, precision=highest))
    return live * (resid + ffn_out)

def reference(tokens, run_counts, seq_lengths, first_gain, in_weight, conv_weight, out_weight, second_gain, gate_weight, up_weight, down_weight, cotangent):
    tables = slot_tables(run_counts, seq_lengths)
    params = (tokens, first_gain, in_weight, conv_weight, out_weight, second_gain, gate_weight, up_weight, down_weight)
    params = tuple((item.astype(jnp.float32) for item in params))
    result, pullback = jax.vjp(lambda *items: forward_block(tables, *items), *params)
    grads = pullback(cotangent.astype(jnp.float32))
    return (result.astype(jnp.bfloat16), grads[0], grads[1], grads[2], grads[3], grads[4], grads[5], grads[6], grads[7], grads[8])
```

```python
import functools

import jax
import jax.numpy as jnp
from jax import lax
from jax.experimental import pallas as pl
from jax.experimental.pallas import tpu as pltpu
from jax.sharding import PartitionSpec as P

epsilon = 1e-05
MESH = pl.DeviceIdType.MESH
bf16, f32 = jnp.bfloat16, jnp.float32
SIDE = 4
RING = (1, 3, 2)
COPIES = 256


def dot(a, b):
    return lax.dot_general(a, b, (((1,), (0,)), ((), ())), preferred_element_type=f32)


def dot_nt(a, b):
    return lax.dot_general(a, b, (((1,), (1,)), ((), ())), preferred_element_type=f32)


def wrap(i):
    return lax.rem(i, SIDE)


def total(values):
    return functools.reduce(lambda a, b: a + b, values)


def kernel(
    tokens, run_counts, seq_lengths, first_gain, in_weight, conv_weight, out_weight, second_gain,
    gate_weight, up_weight, down_weight, cotangent,
    block_out, input_grad, first_gain_grad, in_grad, conv_grad, out_grad, second_gain_grad,
    gate_grad, up_grad, down_grad,
    in_b, out_b, gate_b, up_b, down_b,
    x_g, cot_g, r1_g, gh2_g, gains,
    o_s, o_r, gh2_s, gh2_r, ffo_s, ffo_r, gh1_s, gh1_r, dots,
    in_p, out_p, gate_p, up_p, down_p,
    in_1, out_1, gate_1, up_1, down_1,
    in_2a, in_2b, out_2a, out_2b, gate_2, up_2, down_2a, down_2b,
    in_3, out_3, gate_3, up_3, down_3,
    out_t, down_t,
    h1, h2, h1_t, h2_t, hid, hid_t, g_gate_ref, g_up, g_hid, g_proj, z_t, go,
    b_s, c_s, x_s, conv_s, tap1_s, tap2_s, r1_s, gr1_s, own_s, ffo_own, rs1_s,
    halo_s, halo_r, back_s, back_r, vec_a, vec_b, vec_x, vec_y,
    send, recv,
):
    row, z = lax.axis_index("row"), lax.axis_index("col")
    x, y, k = row // (2 * SIDE), wrap(row // 2), lax.rem(row, 2)
    slots, width = tokens.shape
    rows = 2 * SIDE * SIDE

    def at(x_to, y_to, k_to, z_to):
        return ((wrap(x_to) * SIDE + wrap(y_to)) * 2 + k_to, wrap(z_to))

    def x_peer(d):
        return at(x + d, y, k, z)

    def y_peer(d):
        return at(x, y + d, k, z)

    def z_peer(d):
        return (row, wrap(z + d))

    sibling = (row + 1 - 2 * k, z)
    mirror = at(z, y, k, x)
    next_row, last_row = (lax.rem(row + 1, rows), z), (lax.rem(row + rows - 1, rows), z)

    barrier = pltpu.get_barrier_semaphore()
    peers = [f(d) for f in (x_peer, y_peer, z_peer) for d in RING] + [next_row, last_row]
    for peer in peers:
        pl.semaphore_signal(barrier, inc=1, device_id=peer, device_id_type=MESH)

    @pl.when(x != z)
    def _():
        pl.semaphore_signal(barrier, inc=1, device_id=mirror, device_id_type=MESH)

    slot = lax.broadcasted_iota(jnp.int32, (slots, 1), 0)
    count = run_counts[row]
    offset = total([jnp.where(q < row, run_counts[q], 0) for q in range(rows)])
    position = offset + slot
    is_live = slot < count
    start, seq_start = 0, jnp.zeros((slots, 1), jnp.int32)
    for q in range(seq_lengths.shape[0]):
        seq_start = jnp.maximum(seq_start, jnp.where(position >= start, start, 0))
        start = start + seq_lengths[q]
    valid1 = is_live & (position - 1 >= seq_start)
    valid2 = is_live & (position - 2 >= seq_start)

    x_g[z] = tokens[...]
    cot_g[z] = jnp.where(is_live, cotangent[...].astype(f32), 0.0).astype(bf16)
    gains[z, 0:1, :] = first_gain[...].astype(f32)
    gains[z, 1:2, :] = second_gain[...].astype(f32)
    gains[z, 2:8, :] = jnp.zeros((6, width), f32)
    for p in range(3):
        in_b[x, y, k, :, p * width : (p + 1) * width] = in_weight[p]
    gate_b[x, y, k] = gate_weight[...]
    up_b[x, y, k] = up_weight[...]

    @pl.when(x != z)
    def _():
        pl.semaphore_wait(barrier, len(peers) + 1)

    @pl.when(x == z)
    def _():
        pl.semaphore_wait(barrier, len(peers))

    started = []

    def copy(src, dst, to):
        i = len(started)
        c = pltpu.make_async_remote_copy(
            src_ref=src,
            dst_ref=dst,
            send_sem=send.at[i],
            recv_sem=recv.at[i],
            device_id=to,
            device_id_type=MESH,
        )
        started.append(c)
        return c

    def launch(src, dst, to):
        c = copy(src, dst, to)
        c.start()
        return c

    def arrive(copies):
        for c in copies:
            c.wait_recv()

    def gather_z(buf):
        return [launch(buf.at[z], buf.at[z], z_peer(d)) for d in RING]

    class Gather:
        def __init__(self, buf, first, cols=None):
            self.buf, self.first = buf, first
            self.cols = slice(None) if cols is None else pl.ds(*cols)

        def ring_one(self):
            own = self.buf.at[x, y, k, :, self.cols]
            peer = x_peer if self.first == "x" else y_peer
            self.pending = [launch(own, own, peer(d)) for d in RING]

        def ring_two(self):
            arrive(self.pending)
            if self.first == "x":
                part, peer = self.buf.at[:, y, k, :, self.cols], y_peer
            else:
                part, peer = self.buf.at[x, :, k, :, self.cols], x_peer
            self.pending = [launch(part, part, peer(d)) for d in RING]

        def core(self):
            arrive(self.pending)
            part = self.buf.at[:, :, k, :, self.cols]
            self.pending = [launch(part, part, sibling)]

        def done(self):
            arrive(self.pending)

    class Scatter:
        def __init__(self, partial, one, parts, three):
            self.partial, self.one, self.parts, self.three = partial, one, parts, three

        def core(self):
            self.pending = [launch(self.partial.at[:, :, 1 - k], self.one, sibling)]

        def ring_one(self):
            arrive(self.pending)
            one, partial = self.one, self.partial

            @pl.loop(0, SIDE * SIDE)
            def _(i):
                a, b = i // SIDE, wrap(i)
                one[a, b] = (partial[a, b, k].astype(f32) + one[a, b].astype(f32)).astype(bf16)

            self.pending = []
            for two, first, cols in self.parts:
                cs = pl.ds(*cols)
                sent = []
                for d in RING:
                    if first == "x":
                        part, peer, me = one.at[wrap(x + d), :, :, cs], x_peer(d), x
                    else:
                        part, peer, me = one.at[:, wrap(y + d), :, cs], y_peer(d), y
                    sent.append(launch(part, two.at[me], peer))
                self.pending.append(sent)
                if first == "x":
                    two[x] = one[x, :, :, cs]
                else:
                    two[y] = one[:, y, :, cs]

        def ring_two(self):
            later = []
            for (two, first, cols), sent in zip(self.parts, self.pending):
                arrive(sent)
                me = x if first == "x" else y

                @pl.loop(0, SIDE)
                def _(j):
                    two[me, j] = total([two[s, j].astype(f32) for s in range(SIDE)]).astype(bf16)

                cs = pl.ds(*cols)
                for d in RING:
                    if first == "x":
                        part, peer, to = two.at[x, wrap(y + d)], y_peer(d), y
                    else:
                        part, peer, to = two.at[y, wrap(x + d)], x_peer(d), x
                    later.append(launch(part, self.three.at[to, :, cs], peer))
                if first == "x":
                    self.three[y, :, cs] = two[x, y]
                else:
                    self.three[x, :, cs] = two[y, x]
            self.pending = later

        def done(self):
            arrive(self.pending)
            return total([self.three[s].astype(f32) for s in range(SIDE)])

    got_x = gather_z(x_g) + gather_z(gains)
    in_half = in_b.shape[-1] // 2
    g_in = [Gather(in_b, "x", (0, in_half)), Gather(in_b, "y", (in_half, in_half))]
    for g in g_in:
        g.ring_one()
    swap_out = copy(out_weight, out_b.at[z, y, k], mirror)
    swap_down = copy(down_weight, down_b.at[z, y, k], mirror)

    @pl.when(x != z)
    def _():
        swap_out.start()
        swap_down.start()

    @pl.when(x == z)
    def _():
        out_b[x, y, k] = out_weight[...]
        down_b[x, y, k] = down_weight[...]

    for g in g_in:
        g.ring_two()

    @pl.when(x != z)
    def _():
        swap_out.wait_recv()
        swap_down.wait_recv()

    half = width // 2
    g_out = [Gather(out_b, "x", (0, half)), Gather(out_b, "y", (half, half))]
    g_down = [Gather(down_b, "x", (0, half)), Gather(down_b, "y", (half, half))]
    w_gate, w_up = Gather(gate_b, "x"), Gather(up_b, "y")
    for g in g_out:
        g.ring_one()
    w_gate.ring_one()
    w_up.ring_one()
    got_cot = gather_z(cot_g)

    arrive(got_x)
    features = SIDE * width
    squares = total([jnp.sum(jnp.square(x_g[i].astype(f32)), axis=1, keepdims=True) for i in range(SIDE)])
    rs1_s[...] = lax.rsqrt(squares / features + epsilon)
    for i in range(SIDE):
        h = ((x_g[i].astype(f32) * rs1_s[...]) * gains[i, 0:1, :]).astype(bf16)
        h1[:, i * width : (i + 1) * width] = h
    for g in g_in:
        g.core()
    for g in g_out:
        g.ring_two()
    w_gate.ring_two()
    w_up.ring_two()
    for g in g_down:
        g.ring_one()
    for i in range(SIDE):
        h1_t[i] = h1[:, i * width : (i + 1) * width].T

    for g in g_in:
        g.done()
    for p, ref in enumerate((b_s, c_s, x_s)):
        w = in_b[:, :, :, :, p * width : (p + 1) * width].reshape(features, width)
        ref[...] = dot(h1[...], w)
    u = (b_s[...] * x_s[...]).astype(bf16).astype(f32)
    halo_s[...] = jnp.zeros(halo_s.shape, f32)
    halo_s[0:1, :] = jnp.sum(jnp.where(slot == count - 2, u, 0.0), axis=0, keepdims=True)
    halo_s[1:2, :] = jnp.sum(jnp.where(slot == count - 1, u, 0.0), axis=0, keepdims=True)
    got_halo = launch(halo_s, halo_r, next_row)
    for g in g_out:
        g.core()
    taps = conv_weight[...].astype(f32)
    tap1 = pltpu.roll(u, 1, 0)
    tap2 = pltpu.roll(u, 2, 0)
    for g in g_out:
        g.done()
    got_halo.wait_recv()
    halo = halo_r[...]
    tap1 = jnp.where(valid1, jnp.where(slot == 0, halo[1:2], tap1), 0.0)
    tap2 = jnp.where(valid2, jnp.where(slot == 0, halo[0:1], jnp.where(slot == 1, halo[1:2], tap2)), 0.0)
    tap1_s[...] = tap1
    tap2_s[...] = tap2
    conv = taps[0:1] * u + taps[1:2] * tap1 + taps[2:3] * tap2
    conv_s[...] = conv
    mixed = (c_s[...] * conv).astype(bf16)
    z_t[...] = mixed.T

    got_o = []
    for d in RING:
        i = wrap(z + d)
        o_s[i] = dot(mixed, out_b[i].reshape(width, width)).astype(bf16)
        got_o.append(launch(o_s.at[i], o_r.at[z], z_peer(d)))
    r1_s[...] = tokens[...].astype(f32) + dot(mixed, out_b[z].reshape(width, width))
    for g in g_down:
        g.ring_two()
    arrive(got_o)
    r1 = r1_s[...] + total([o_r[wrap(z + d)].astype(f32) for d in RING])
    r1_s[...] = r1
    r1_g[z] = r1.astype(bf16)
    got_r1 = gather_z(r1_g)

    arrive(got_cot)
    w_gate.core()
    w_up.core()
    for g in g_down:
        g.core()
    for g in g_down:
        g.done()
    units = hid.shape[1]
    g_hid[...] = total([dot_nt(cot_g[i], down_b[i].reshape(units, width)) for i in range(SIDE)])

    arrive(got_r1)
    squares = total([jnp.sum(jnp.square(r1_g[i].astype(f32)), axis=1, keepdims=True) for i in range(SIDE)])
    rs2 = lax.rsqrt(squares / features + epsilon)
    for i in range(SIDE):
        h = ((r1_g[i].astype(f32) * rs2) * gains[i, 1:2, :]).astype(bf16)
        h2[:, i * width : (i + 1) * width] = h

    w_gate.done()
    w_up.done()
    tile = units // 3
    for n in range(3):
        cs = slice(n * tile, (n + 1) * tile)
        gate = dot(h2[...], gate_b[:, :, :, :, cs].reshape(features, tile))
        up = dot(h2[...], up_b[:, :, :, :, cs].reshape(features, tile))
        sigma = jax.nn.sigmoid(gate)
        swish = gate * sigma
        grad = g_hid[:, cs]
        hid[:, cs] = (swish * up).astype(bf16)
        g_gate_n = grad * up * sigma * (1.0 + gate * (1.0 - sigma))
        g_gate_ref[:, cs] = g_gate_n.astype(bf16)
        g_up[:, cs] = (grad * swish).astype(bf16)

    def h2_part(i):
        return dot_nt(g_gate_ref[...], gate_b[i].reshape(width, units)) + dot_nt(
            g_up[...], up_b[i].reshape(width, units)
        )

    got_gh2 = []
    for d in RING:
        i = wrap(z + d)
        gh2_s[i] = h2_part(i).astype(bf16)
        got_gh2.append(launch(gh2_s.at[i], gh2_r.at[z], z_peer(d)))
    own_s[...] = h2_part(z)
    hid_t[...] = hid[...].T

    @pl.loop(0, SIDE)
    def _(i):
        down_p[i] = dot(hid_t[...], cot_g[i]).astype(bf16).reshape(down_p.shape[1:])

    s_down = Scatter(down_p, down_1, [(down_2a, "x", (0, half)), (down_2b, "y", (half, half))], down_3)
    s_down.core()
    for i in range(SIDE):
        h2_t[i] = h2[:, i * width : (i + 1) * width].T

    @pl.loop(0, SIDE)
    def _(i):
        gate_p[i] = dot(h2_t[i], g_gate_ref[...]).astype(bf16).reshape(gate_p.shape[1:])

    s_gate = Scatter(gate_p, gate_1, [(gate_2, "x", (0, units))], gate_3)
    s_gate.core()
    arrive(got_gh2)
    gh2_g[z] = (own_s[...] + total([gh2_r[wrap(z + d)].astype(f32) for d in RING])).astype(bf16)
    got_gh2 = gather_z(gh2_g)
    s_down.ring_one()

    @pl.loop(0, SIDE)
    def _(i):
        up_p[i] = dot(h2_t[i], g_up[...]).astype(bf16).reshape(up_p.shape[1:])

    s_up = Scatter(up_p, up_1, [(up_2, "y", (0, units))], up_3)
    s_up.core()
    s_gate.ring_one()
    s_up.ring_one()

    arrive(got_gh2)
    mean2 = total(
        [
            jnp.sum(gh2_g[i].astype(f32) * gains[i, 1:2, :] * (r1_g[i].astype(f32) * rs2), axis=1, keepdims=True)
            for i in range(SIDE)
        ]
    ) / features

    def r1_grad(i):
        n2 = r1_g[i].astype(f32) * rs2
        return cot_g[i].astype(f32) + rs2 * (gh2_g[i].astype(f32) * gains[i, 1:2, :] - n2 * mean2)

    for i in range(SIDE):
        go[i] = r1_grad(i).astype(bf16)
    gr1_s[...] = r1_grad(z)
    vec_a[...] = jnp.zeros(vec_a.shape, f32)
    vec_a[0:1, :] = jnp.sum(gh2_g[z].astype(f32) * (r1_g[z].astype(f32) * rs2), axis=0, keepdims=True)

    g_z = total([dot_nt(go[i], out_b[i].reshape(width, width)) for i in range(SIDE)])
    g_c = g_z * conv_s[...]
    g_v = g_z * c_s[...]
    u = (b_s[...] * x_s[...]).astype(bf16).astype(f32)
    into1 = jnp.where(valid1, taps[1:2] * g_v, 0.0)
    into2 = jnp.where(valid2, taps[2:3] * g_v, 0.0)
    back_s[...] = jnp.zeros(back_s.shape, f32)
    back_s[0:1, :] = into2[0:1, :]
    back_s[1:2, :] = into1[0:1, :] + into2[1:2, :]
    got_back = launch(back_s, back_r, last_row)
    vec_a[1:2, :] = jnp.sum(g_v * u, axis=0, keepdims=True)
    vec_a[2:3, :] = jnp.sum(g_v * tap1_s[...], axis=0, keepdims=True)
    vec_a[3:4, :] = jnp.sum(g_v * tap2_s[...], axis=0, keepdims=True)
    g_u = taps[0:1] * g_v
    g_u = g_u + jnp.where(slot < slots - 1, pltpu.roll(into1, slots - 1, 0), 0.0)
    g_u = g_u + jnp.where(slot < slots - 2, pltpu.roll(into2, slots - 2, 0), 0.0)
    got_back.wait_recv()
    back = back_r[...]
    g_u = g_u + jnp.where(slot == count - 2, back[0:1], 0.0) + jnp.where(slot == count - 1, back[1:2], 0.0)
    g_proj[:, 0:width] = (g_u * x_s[...]).astype(bf16)
    g_proj[:, width : 2 * width] = g_c.astype(bf16)
    g_proj[:, 2 * width : 3 * width] = (g_u * b_s[...]).astype(bf16)

    for i in range(SIDE):
        in_p[i] = dot(h1_t[i], g_proj[...]).astype(bf16).reshape(in_p.shape[1:])
    s_in = Scatter(in_p, in_1, [(in_2a, "x", (0, in_half)), (in_2b, "y", (in_half, in_half))], in_3)
    s_in.core()

    ones = jnp.ones((8, width), bf16)

    def h1_part(i):
        part = dot_nt(g_proj[...], in_b[i].reshape(width, 3 * width))
        n1 = x_g[i].astype(f32) * rs1_s[...]
        return part, dot_nt(ones, (part * gains[i, 0:1, :] * n1).astype(bf16))

    got_gh1, along = [], []
    for d in RING:
        i = wrap(z + d)
        part, one = h1_part(i)
        along.append(one)
        gh1_s[i] = part.astype(bf16)
        got_gh1.append(launch(gh1_s.at[i], gh1_r.at[z], z_peer(d)))
    part, one = h1_part(z)
    own_s[...] = part
    dots[z] = total(along) + one
    got_gh1 += gather_z(dots)
    s_in.ring_one()

    for i in range(SIDE):
        out_p[i] = dot(z_t[...], go[i]).astype(bf16).reshape(out_p.shape[1:])
    s_out = Scatter(out_p, out_1, [(out_2a, "x", (0, half)), (out_2b, "y", (half, half))], out_3)
    s_out.core()

    got_ffo = []
    for d in RING:
        i = wrap(z + d)
        ffo_s[i] = dot(hid[...], down_b[i].reshape(units, width)).astype(bf16)
        got_ffo.append(launch(ffo_s.at[i], ffo_r.at[z], z_peer(d)))
    ffo_own[...] = r1_s[...] + dot(hid[...], down_b[z].reshape(units, width))

    s_down.ring_two()
    s_out.ring_one()
    s_gate.ring_two()
    s_up.ring_two()

    arrive(got_gh1)
    gh1 = own_s[...] + total([gh1_r[wrap(z + d)].astype(f32) for d in RING])
    mean1 = total([dots[i] for i in range(SIDE)]).T[:, 0:1] / features
    n1 = tokens[...].astype(f32) * rs1_s[...]
    input_grad[...] = gr1_s[...] + rs1_s[...] * (gh1 * gains[z, 0:1, :] - n1 * mean1)
    vec_a[4:5, :] = jnp.sum(gh1 * n1, axis=0, keepdims=True)
    got_vec = launch(vec_a, vec_b, sibling)

    down_t[...] = s_down.done()
    back_down = copy(down_t, down_grad, mirror)

    @pl.when(x != z)
    def _():
        back_down.start()

    @pl.when(x == z)
    def _():
        down_grad[...] = down_t[...]

    s_in.ring_two()
    s_out.ring_two()
    got_vec.wait_recv()
    vec_x[x] = vec_a[...] + vec_b[...]
    got_vec = [launch(vec_x.at[x], vec_x.at[x], x_peer(d)) for d in RING]
    gate_grad[...] = s_gate.done()
    up_grad[...] = s_up.done()
    arrive(got_vec)
    vec_y[y] = total([vec_x[s] for s in range(SIDE)])
    got_vec = [launch(vec_y.at[y], vec_y.at[y], y_peer(d)) for d in RING]
    out_t[...] = s_out.done()
    back_out = copy(out_t, out_grad, mirror)

    @pl.when(x != z)
    def _():
        back_out.start()

    @pl.when(x == z)
    def _():
        out_grad[...] = out_t[...]

    arrive(got_ffo)
    ffo = ffo_own[...] + total([ffo_r[wrap(z + d)].astype(f32) for d in RING])
    block_out[...] = jnp.where(is_live, ffo, 0.0).astype(bf16)
    in_sum = s_in.done()
    for p in range(3):
        in_grad[p] = in_sum[:, p * width : (p + 1) * width]
    arrive(got_vec)
    vec = total([vec_y[s] for s in range(SIDE)])
    second_gain_grad[...] = vec[0:1]
    conv_grad[...] = vec[1:4]
    first_gain_grad[...] = vec[4:5]

    mirrored = (swap_out, swap_down, back_down, back_out)

    @pl.when(x != z)
    def _():
        arrive((back_down, back_out))
        for c in mirrored:
            c.wait_send()

    for c in started:
        if not any(c is m for m in mirrored):
            c.wait_send()


def body(
    tokens,
    run_counts,
    seq_lengths,
    first_gain,
    in_weight,
    conv_weight,
    out_weight,
    second_gain,
    gate_weight,
    up_weight,
    down_weight,
    cotangent,
):
    slots, width = tokens.shape
    wide = in_weight.shape[0]
    units, deep = gate_weight.shape[1], down_weight.shape[0]
    three = 3 * width
    features = SIDE * width

    def vm(*shape, dtype=bf16):
        return pltpu.VMEM(shape, dtype)

    gathered = [
        vm(SIDE, SIDE, 2, r, w)
        for r, w in ((wide, three), (wide, width), (wide, units), (wide, units), (deep, width))
    ]
    by_col = [vm(SIDE, slots, width) for _ in range(4)] + [vm(SIDE, 8, width, dtype=f32)]
    summed = [vm(SIDE, slots, width) for _ in range(8)] + [vm(SIDE, 8, slots, dtype=f32)]
    ones = [
        vm(SIDE, SIDE, r, w)
        for r, w in ((wide, three), (wide, width), (wide, units), (wide, units), (deep, width))
    ]
    twos = [
        vm(SIDE, SIDE, r, w)
        for r, w in (
            (wide, three // 2), (wide, three // 2), (wide, width // 2), (wide, width // 2),
            (wide, units), (wide, units), (deep, width // 2), (deep, width // 2),
        )
    ]
    threes = [
        vm(SIDE, r, w)
        for r, w in ((wide, three), (wide, width), (wide, units), (wide, units), (deep, width))
    ]
    turned = [vm(wide, width, dtype=f32), vm(deep, width, dtype=f32)]
    own = [
        vm(slots, features), vm(slots, features), vm(SIDE, width, slots), vm(SIDE, width, slots),
        vm(slots, units), vm(units, slots), vm(slots, units), vm(slots, units),
        vm(slots, units, dtype=f32), vm(slots, three), vm(width, slots), vm(SIDE, slots, width),
    ]
    own += [vm(slots, width, dtype=f32) for _ in range(10)] + [vm(slots, 1, dtype=f32)]
    small = [vm(8, width, dtype=f32) for _ in range(6)] + [vm(SIDE, 8, width, dtype=f32) for _ in range(2)]
    scratch = gathered + by_col + summed + gathered + ones + twos + threes + turned + own + small
    scratch += [pltpu.SemaphoreType.DMA((COPIES,)), pltpu.SemaphoreType.DMA((COPIES,))]

    vmem, smem = pl.BlockSpec(memory_space=pltpu.VMEM), pl.BlockSpec(memory_space=pltpu.SMEM)

    def out(*shape, dtype=f32):
        return jax.ShapeDtypeStruct(shape, dtype)

    (block_out, input_grad, first_grad, in_grad, conv_grad, out_grad, second_grad, gate_grad, up_grad, down_grad) = (
        pl.pallas_call(
            kernel,
            out_shape=(
                out(slots, width, dtype=bf16), out(slots, width), out(1, width), out(3, wide, width), out(3, width),
                out(wide, width), out(1, width), out(wide, units), out(wide, units), out(deep, width),
            ),
            in_specs=[vmem, smem, smem] + [vmem] * 9,
            out_specs=(vmem,) * 10,
            scratch_shapes=scratch,
            compiler_params=pltpu.CompilerParams(
                collective_id=0, has_side_effects=True, vmem_limit_bytes=60 * 2**20
            ),
            name="block",
        )(
            tokens, run_counts, seq_lengths, first_gain.reshape(1, width), in_weight.transpose(1, 0, 2), conv_weight,
            out_weight, second_gain.reshape(1, width), gate_weight, up_weight, down_weight, cotangent,
        )
    )
    return (
        block_out,
        input_grad,
        first_grad.reshape(width),
        in_grad.transpose(1, 0, 2),
        conv_grad,
        out_grad,
        second_grad.reshape(width),
        gate_grad,
        up_grad,
        down_grad,
    )


def solution(mesh):
    return jax.shard_map(
        body,
        mesh=mesh,
        in_specs=(
            P("row", "col"),
            P(),
            P(),
            P("col"),
            P("row", None, "col"),
            P(None, "col"),
            P("row", "col"),
            P("col"),
            P("row", "col"),
            P("row", "col"),
            P("row", "col"),
            P("row", "col"),
        ),
        out_specs=(
            P("row", "col"),
            P("row", "col"),
            P("col"),
            P("row", None, "col"),
            P(None, "col"),
            P("row", "col"),
            P("col"),
            P("row", "col"),
            P("row", "col"),
            P("row", "col"),
        ),
        check_vma=False,
    )
```

```python
import functools

import jax
import jax.numpy as jnp
from jax import lax
from jax.experimental import pallas as pl
from jax.experimental.pallas import tpu as pltpu
from jax.sharding import PartitionSpec as P

epsilon = 1e-05
MESH = pl.DeviceIdType.MESH
bf16, f32 = jnp.bfloat16, jnp.float32
SIDE = 4
RING = (1, 3, 2)
COPIES = 256


def dot(a, b):
    return lax.dot_general(a, b, (((1,), (0,)), ((), ())), preferred_element_type=f32)


def dot_nt(a, b):
    return lax.dot_general(a, b, (((1,), (1,)), ((), ())), preferred_element_type=f32)


def wrap(i):
    return lax.rem(i, SIDE)


def total(values):
    return functools.reduce(lambda a, b: a + b, values)


def kernel(
    tokens, run_counts, seq_lengths, first_gain, in_weight, conv_weight, out_weight, second_gain,
    gate_weight, up_weight, down_weight, cotangent,
    block_out, input_grad, first_gain_grad, in_grad, conv_grad, out_grad, second_gain_grad,
    gate_grad, up_grad, down_grad,
    in_b, out_b, gate_b, up_b, down_b,
    x_g, cot_g, r1_g, gh2_g, gains,
    o_s, o_r, gh2_s, gh2_r, ffo_s, ffo_r, gh1_s, gh1_r, dots,
    in_p, out_p, gate_p, up_p, down_p,
    in_1, out_1, gate_1, up_1, down_1,
    in_2a, in_2b, out_2, gate_2, up_2, down_2a, down_2b,
    in_3, out_3, gate_3, up_3, down_3,
    out_t, down_t, out_i, down_i,
    h1, h2, h1_t, h2_t, hid, hid_t, g_gate_ref, g_up, g_hid, g_proj, z_t, go,
    b_s, c_s, x_s, conv_s, tap1_s, tap2_s, r1_s, gr1_s, own_s, ffo_own, rs1_s,
    tail_s, back_s, back_r, vec_a, vec_b, vec_x, vec_y, tail_g,
    send, recv, brought,
):
    row, z = lax.axis_index("row"), lax.axis_index("col")
    x, y, k = row // (2 * SIDE), wrap(row // 2), lax.rem(row, 2)
    slots, width = tokens.shape
    rows = 2 * SIDE * SIDE

    def at(x_to, y_to, k_to, z_to):
        return ((wrap(x_to) * SIDE + wrap(y_to)) * 2 + k_to, wrap(z_to))

    def x_peer(d):
        return at(x + d, y, k, z)

    def y_peer(d):
        return at(x, y + d, k, z)

    def z_peer(d):
        return (row, wrap(z + d))

    sibling = (row + 1 - 2 * k, z)
    mirror = at(z, y, k, x)
    next_row, last_row = (lax.rem(row + 1, rows), z), (lax.rem(row + rows - 1, rows), z)

    local = []

    def bring(src, dst):
        c = pltpu.make_async_copy(src, dst, brought.at[len(local)])
        local.append(c)
        c.start()

    for p in range(3):
        bring(in_weight.at[p], in_b.at[x, y, k, :, p * width : (p + 1) * width])
    bring(tokens, x_g.at[z])
    bring(gate_weight, gate_b.at[x, y, k])
    bring(up_weight, up_b.at[x, y, k])
    bring(cotangent, cot_g.at[z])
    bring(out_weight, out_i)
    bring(down_weight, down_i)
    barrier = pltpu.get_barrier_semaphore()
    peers = [f(d) for f in (x_peer, y_peer, z_peer) for d in RING] + [next_row, last_row]
    for peer in peers:
        pl.semaphore_signal(barrier, inc=1, device_id=peer, device_id_type=MESH)

    @pl.when(x != z)
    def _():
        pl.semaphore_signal(barrier, inc=1, device_id=mirror, device_id_type=MESH)

    gains[z, 0:1, :] = first_gain[...].astype(f32).reshape(1, width)
    gains[z, 1:2, :] = second_gain[...].astype(f32).reshape(1, width)
    gains[z, 2:8, :] = jnp.zeros((6, width), f32)
    for c in local:
        c.wait()

    @pl.when(x != z)
    def _():
        pl.semaphore_wait(barrier, len(peers) + 1)

    @pl.when(x == z)
    def _():
        pl.semaphore_wait(barrier, len(peers))

    started = []

    def copy(src, dst, to):
        i = len(started)
        c = pltpu.make_async_remote_copy(
            src_ref=src,
            dst_ref=dst,
            send_sem=send.at[i],
            recv_sem=recv.at[i],
            device_id=to,
            device_id_type=MESH,
        )
        started.append(c)
        return c

    def launch(src, dst, to):
        c = copy(src, dst, to)
        c.start()
        return c

    def arrive(copies):
        for c in copies:
            c.wait_recv()

    def gather_z(buf):
        return [launch(buf.at[z], buf.at[z], z_peer(d)) for d in RING]

    class Gather:
        def __init__(self, buf, first, cols=None):
            self.buf, self.first = buf, first
            self.cols = slice(None) if cols is None else pl.ds(*cols)

        def ring_one(self):
            own = self.buf.at[x, y, k, :, self.cols]
            peer = x_peer if self.first == "x" else y_peer
            self.pending = [launch(own, own, peer(d)) for d in RING]

        def ring_two(self):
            arrive(self.pending)
            if self.first == "x":
                part, peer = self.buf.at[:, y, k, :, self.cols], y_peer
            else:
                part, peer = self.buf.at[x, :, k, :, self.cols], x_peer
            self.pending = [launch(part, part, peer(d)) for d in RING]

        def core(self):
            arrive(self.pending)
            part = self.buf.at[:, :, k, :, self.cols]
            self.pending = [launch(part, part, sibling)]

        def done(self):
            arrive(self.pending)

    class Scatter:
        def __init__(self, partial, one, parts, three):
            self.partial, self.one, self.parts, self.three = partial, one, parts, three

        def core(self):
            self.pending = [launch(self.partial.at[:, :, 1 - k], self.one, sibling)]

        def ring_one(self):
            arrive(self.pending)
            one, partial = self.one, self.partial

            @pl.loop(0, SIDE * SIDE)
            def _(i):
                a, b = i // SIDE, wrap(i)
                one[a, b] = (partial[a, b, k].astype(f32) + one[a, b].astype(f32)).astype(bf16)

            self.pending = []
            for two, first, cols in self.parts:
                cs = pl.ds(*cols)
                sent = []
                for d in RING:
                    if first == "x":
                        part, peer, me = one.at[wrap(x + d), :, :, cs], x_peer(d), x
                    else:
                        part, peer, me = one.at[:, wrap(y + d), :, cs], y_peer(d), y
                    sent.append(launch(part, two.at[me], peer))
                self.pending.append(sent)
                if first == "x":
                    two[x] = one[x, :, :, cs]
                else:
                    two[y] = one[:, y, :, cs]

        def ring_two(self):
            later = []
            for (two, first, cols), sent in zip(self.parts, self.pending):
                arrive(sent)
                me = x if first == "x" else y

                @pl.loop(0, SIDE)
                def _(j):
                    two[me, j] = total([two[s, j].astype(f32) for s in range(SIDE)]).astype(bf16)

                cs = pl.ds(*cols)
                for d in RING:
                    if first == "x":
                        part, peer, to = two.at[x, wrap(y + d)], y_peer(d), y
                    else:
                        part, peer, to = two.at[y, wrap(x + d)], x_peer(d), x
                    later.append(launch(part, self.three.at[to, :, cs], peer))
                if first == "x":
                    self.three[y, :, cs] = two[x, y]
                else:
                    self.three[x, :, cs] = two[y, x]
            self.pending = later

        def done(self):
            arrive(self.pending)
            return total([self.three[s].astype(f32) for s in range(SIDE)])

    in_half = in_b.shape[-1] // 2
    half = width // 2
    g_in = [Gather(in_b, "x", (0, in_half)), Gather(in_b, "y", (in_half, in_half))]
    g_out = Gather(out_b, "x")
    g_down = [Gather(down_b, "x", (0, half)), Gather(down_b, "y", (half, half))]
    w_gate, w_up = Gather(gate_b, "x"), Gather(up_b, "y")
    for g in g_in:
        g.ring_one()
    got_x = gather_z(x_g) + gather_z(gains)

    slot = lax.broadcasted_iota(jnp.int32, (slots, 1), 0)
    count = run_counts[row]
    offset = total([jnp.where(q < row, run_counts[q], 0) for q in range(rows)])
    position = offset + slot
    is_live = slot < count
    start, seq_start = 0, jnp.zeros((slots, 1), jnp.int32)
    for q in range(seq_lengths.shape[0]):
        seq_start = jnp.maximum(seq_start, jnp.where(position >= start, start, 0))
        start = start + seq_lengths[q]
    valid1 = is_live & (position - 1 >= seq_start)
    valid2 = is_live & (position - 2 >= seq_start)


    def last_two(values):
        one = jnp.sum(jnp.where(slot == count - 2, values, 0.0), axis=0, keepdims=True)
        two = jnp.sum(jnp.where(slot == count - 1, values, 0.0), axis=0, keepdims=True)
        return one, two

    tail_s[...] = jnp.zeros(tail_s.shape, f32)
    tail_s[0:1, :], tail_s[1:2, :] = last_two(x_g[z].astype(f32))
    got_tail = launch(tail_s, tail_g.at[z], next_row)
    swap_out = copy(out_i, out_b.at[z, y, k], mirror)
    swap_down = copy(down_i, down_b.at[z, y, k], mirror)

    @pl.when(x != z)
    def _():
        swap_out.start()
        swap_down.start()

    @pl.when(x == z)
    def _():
        out_b[x, y, k] = out_i[...]
        down_b[x, y, k] = down_i[...]

    for g in g_in:
        g.ring_two()
    got_tail.wait_recv()
    got_tail = gather_z(tail_g)

    @pl.when(x != z)
    def _():
        swap_out.wait_recv()
        swap_down.wait_recv()

    g_out.ring_one()
    w_gate.ring_one()
    w_up.ring_one()
    for g in g_down:
        g.ring_one()
    cot_g[z] = jnp.where(is_live, cot_g[z].astype(f32), 0.0).astype(bf16)
    got_cot = gather_z(cot_g)

    arrive(got_x)
    g_out.ring_two()
    features = SIDE * width

    def scale(values):
        return lax.rsqrt(total([jnp.sum(jnp.square(v), axis=1, keepdims=True) for v in values]) / features + epsilon)

    rs1_s[...] = scale([x_g[i].astype(f32) for i in range(SIDE)])
    for i in range(SIDE):
        h = ((x_g[i].astype(f32) * rs1_s[...]) * gains[i, 0:1, :]).astype(bf16)
        h1[0:slots, i * width : (i + 1) * width] = h
    for g in g_in:
        g.core()
    w_gate.ring_two()
    w_up.ring_two()
    for g in g_down:
        g.ring_two()
    arrive(got_tail)
    tail_scale = scale([tail_g[i] for i in range(SIDE)])
    for i in range(SIDE):
        h = (tail_g[i] * tail_scale) * gains[i, 0:1, :]
        h = jnp.concatenate([h, jnp.zeros(h.shape, f32)], axis=0).astype(bf16)
        h1[slots : slots + 16, i * width : (i + 1) * width] = h
    for i in range(SIDE):
        h1_t[i] = h1[0:slots, i * width : (i + 1) * width].T

    for g in g_in:
        g.done()

    def in_part(p, tokens_of):
        return dot(tokens_of, in_b[:, :, :, :, p * width : (p + 1) * width].reshape(features, width))

    b_all, x_all = in_part(0, h1[...]), in_part(2, h1[...])
    b_s[...], x_s[...] = b_all[0:slots], x_all[0:slots]
    c_s[...] = in_part(1, h1[0:slots, :])
    u_all = (b_all * x_all).astype(bf16).astype(f32)
    u, halo = u_all[0:slots], u_all[slots : slots + 8]
    g_out.core()
    taps = conv_weight[...].astype(f32)
    tap1 = pltpu.roll(u, 1, 0)
    tap2 = pltpu.roll(u, 2, 0)
    tap1 = jnp.where(valid1, jnp.where(slot == 0, halo[1:2], tap1), 0.0)
    tap2 = jnp.where(valid2, jnp.where(slot == 0, halo[0:1], jnp.where(slot == 1, halo[1:2], tap2)), 0.0)
    tap1_s[...] = tap1
    tap2_s[...] = tap2
    conv = taps[0:1] * u + taps[1:2] * tap1 + taps[2:3] * tap2
    conv_s[...] = conv
    mixed = (c_s[...] * conv).astype(bf16)
    z_t[...] = mixed.T
    g_out.done()

    got_o = []
    for d in RING:
        i = wrap(z + d)
        o_s[i] = dot(mixed, out_b[i].reshape(width, width)).astype(bf16)
        got_o.append(launch(o_s.at[i], o_r.at[z], z_peer(d)))
    r1_s[...] = x_g[z].astype(f32) + dot(mixed, out_b[z].reshape(width, width))
    arrive(got_o)
    r1 = r1_s[...] + total([o_r[wrap(z + d)].astype(f32) for d in RING])
    r1_s[...] = r1
    r1_g[z] = r1.astype(bf16)
    got_r1 = gather_z(r1_g)

    arrive(got_cot)
    w_gate.core()
    w_up.core()
    for g in g_down:
        g.core()
    for g in g_down:
        g.done()
    units = hid.shape[1]
    g_hid[...] = total([dot_nt(cot_g[i], down_b[i].reshape(units, width)) for i in range(SIDE)])

    arrive(got_r1)
    rs2 = scale([r1_g[i].astype(f32) for i in range(SIDE)])
    for i in range(SIDE):
        h = ((r1_g[i].astype(f32) * rs2) * gains[i, 1:2, :]).astype(bf16)
        h2[:, i * width : (i + 1) * width] = h

    w_gate.done()
    w_up.done()
    tile = units // 3
    for n in range(3):
        cs = slice(n * tile, (n + 1) * tile)
        gate = dot(h2[...], gate_b[:, :, :, :, cs].reshape(features, tile))
        up = dot(h2[...], up_b[:, :, :, :, cs].reshape(features, tile))
        sigma = jax.nn.sigmoid(gate)
        swish = gate * sigma
        grad = g_hid[:, cs]
        hid[:, cs] = (swish * up).astype(bf16)
        g_gate_n = grad * up * sigma * (1.0 + gate * (1.0 - sigma))
        g_gate_ref[:, cs] = g_gate_n.astype(bf16)
        g_up[:, cs] = (grad * swish).astype(bf16)

    def h2_part(i):
        return dot_nt(g_gate_ref[...], gate_b[i].reshape(width, units)) + dot_nt(
            g_up[...], up_b[i].reshape(width, units)
        )

    got_gh2 = []
    for d in RING:
        i = wrap(z + d)
        gh2_s[i] = h2_part(i).astype(bf16)
        got_gh2.append(launch(gh2_s.at[i], gh2_r.at[z], z_peer(d)))
    own_s[...] = h2_part(z)
    hid_t[...] = hid[...].T

    @pl.loop(0, SIDE)
    def _(i):
        down_p[i] = dot(hid_t[...], cot_g[i]).astype(bf16).reshape(down_p.shape[1:])

    s_down = Scatter(down_p, down_1, [(down_2a, "x", (0, half)), (down_2b, "y", (half, half))], down_3)
    s_down.core()
    for i in range(SIDE):
        h2_t[i] = h2[:, i * width : (i + 1) * width].T

    @pl.loop(0, SIDE)
    def _(i):
        gate_p[i] = dot(h2_t[i], g_gate_ref[...]).astype(bf16).reshape(gate_p.shape[1:])

    s_gate = Scatter(gate_p, gate_1, [(gate_2, "x", (0, units))], gate_3)
    s_gate.core()
    arrive(got_gh2)
    gh2_g[z] = (own_s[...] + total([gh2_r[wrap(z + d)].astype(f32) for d in RING])).astype(bf16)
    got_gh2 = gather_z(gh2_g)
    s_down.ring_one()

    @pl.loop(0, SIDE)
    def _(i):
        up_p[i] = dot(h2_t[i], g_up[...]).astype(bf16).reshape(up_p.shape[1:])

    s_up = Scatter(up_p, up_1, [(up_2, "y", (0, units))], up_3)
    s_up.core()
    s_gate.ring_one()
    s_up.ring_one()

    arrive(got_gh2)
    mean2 = total(
        [
            jnp.sum(gh2_g[i].astype(f32) * gains[i, 1:2, :] * (r1_g[i].astype(f32) * rs2), axis=1, keepdims=True)
            for i in range(SIDE)
        ]
    ) / features

    def r1_grad(i):
        n2 = r1_g[i].astype(f32) * rs2
        return cot_g[i].astype(f32) + rs2 * (gh2_g[i].astype(f32) * gains[i, 1:2, :] - n2 * mean2)

    for i in range(SIDE):
        go[i] = r1_grad(i).astype(bf16)
    gr1_s[...] = r1_grad(z)
    vec_a[...] = jnp.zeros(vec_a.shape, f32)
    vec_a[0:1, :] = jnp.sum(gh2_g[z].astype(f32) * (r1_g[z].astype(f32) * rs2), axis=0, keepdims=True)

    g_z = total([dot_nt(go[i], out_b[i].reshape(width, width)) for i in range(SIDE)])
    g_c = g_z * conv_s[...]
    g_v = g_z * c_s[...]
    u = (b_s[...] * x_s[...]).astype(bf16).astype(f32)
    into1 = jnp.where(valid1, taps[1:2] * g_v, 0.0)
    into2 = jnp.where(valid2, taps[2:3] * g_v, 0.0)
    back_s[...] = jnp.zeros(back_s.shape, f32)
    back_s[0:1, :] = into2[0:1, :]
    back_s[1:2, :] = into1[0:1, :] + into2[1:2, :]
    got_back = launch(back_s, back_r, last_row)
    for i in range(SIDE):
        out_p[i] = dot(z_t[...], go[i]).astype(bf16).reshape(out_p.shape[1:])
    s_out = Scatter(out_p, out_1, [(out_2, "y", (0, width))], out_3)
    s_out.core()
    vec_a[1:2, :] = jnp.sum(g_v * u, axis=0, keepdims=True)
    vec_a[2:3, :] = jnp.sum(g_v * tap1_s[...], axis=0, keepdims=True)
    vec_a[3:4, :] = jnp.sum(g_v * tap2_s[...], axis=0, keepdims=True)
    g_u = taps[0:1] * g_v
    g_u = g_u + jnp.where(slot < slots - 1, pltpu.roll(into1, slots - 1, 0), 0.0)
    g_u = g_u + jnp.where(slot < slots - 2, pltpu.roll(into2, slots - 2, 0), 0.0)
    got_back.wait_recv()
    back = back_r[...]
    g_u = g_u + jnp.where(slot == count - 2, back[0:1], 0.0) + jnp.where(slot == count - 1, back[1:2], 0.0)
    g_proj[:, 0:width] = (g_u * x_s[...]).astype(bf16)
    g_proj[:, width : 2 * width] = g_c.astype(bf16)
    g_proj[:, 2 * width : 3 * width] = (g_u * b_s[...]).astype(bf16)

    for i in range(SIDE):
        in_p[i] = dot(h1_t[i], g_proj[...]).astype(bf16).reshape(in_p.shape[1:])
    s_in = Scatter(in_p, in_1, [(in_2a, "x", (0, in_half)), (in_2b, "y", (in_half, in_half))], in_3)
    s_in.core()

    ones = jnp.ones((8, width), bf16)

    def h1_part(i):
        part = dot_nt(g_proj[...], in_b[i].reshape(width, 3 * width))
        n1 = x_g[i].astype(f32) * rs1_s[...]
        return part, dot_nt(ones, (part * gains[i, 0:1, :] * n1).astype(bf16))

    got_gh1, along = [], []
    for d in RING:
        i = wrap(z + d)
        part, one = h1_part(i)
        along.append(one)
        gh1_s[i] = part.astype(bf16)
        got_gh1.append(launch(gh1_s.at[i], gh1_r.at[z], z_peer(d)))
    part, one = h1_part(z)
    own_s[...] = part
    dots[z] = total(along) + one
    got_gh1 += gather_z(dots)
    s_down.ring_two()
    s_in.ring_one()
    s_out.ring_one()

    got_ffo = []
    for d in RING:
        i = wrap(z + d)
        ffo_s[i] = dot(hid[...], down_b[i].reshape(units, width)).astype(bf16)
        got_ffo.append(launch(ffo_s.at[i], ffo_r.at[z], z_peer(d)))
    ffo_own[...] = r1_s[...] + dot(hid[...], down_b[z].reshape(units, width))

    s_gate.ring_two()
    s_up.ring_two()

    arrive(got_gh1)
    gh1 = own_s[...] + total([gh1_r[wrap(z + d)].astype(f32) for d in RING])
    mean1 = total([dots[i] for i in range(SIDE)]).T[:, 0:1] / features
    n1 = x_g[z].astype(f32) * rs1_s[...]
    input_grad[...] = gr1_s[...] + rs1_s[...] * (gh1 * gains[z, 0:1, :] - n1 * mean1)
    vec_a[4:5, :] = jnp.sum(gh1 * n1, axis=0, keepdims=True)
    got_vec = launch(vec_a, vec_b, sibling)

    down_t[...] = s_down.done()
    back_down = copy(down_t, down_grad, mirror)

    @pl.when(x != z)
    def _():
        back_down.start()

    @pl.when(x == z)
    def _():
        down_grad[...] = down_t[...]

    s_in.ring_two()
    s_out.ring_two()
    got_vec.wait_recv()
    vec_x[x] = vec_a[...] + vec_b[...]
    got_vec = [launch(vec_x.at[x], vec_x.at[x], x_peer(d)) for d in RING]
    gate_grad[...] = s_gate.done()
    up_grad[...] = s_up.done()
    arrive(got_vec)
    vec_y[y] = total([vec_x[s] for s in range(SIDE)])
    got_vec = [launch(vec_y.at[y], vec_y.at[y], y_peer(d)) for d in RING]
    out_t[...] = s_out.done()
    back_out = copy(out_t, out_grad, mirror)

    @pl.when(x != z)
    def _():
        back_out.start()

    @pl.when(x == z)
    def _():
        out_grad[...] = out_t[...]

    arrive(got_ffo)
    ffo = ffo_own[...] + total([ffo_r[wrap(z + d)].astype(f32) for d in RING])
    block_out[...] = jnp.where(is_live, ffo, 0.0).astype(bf16)
    in_sum = s_in.done()
    for p in range(3):
        in_grad[p] = in_sum[:, p * width : (p + 1) * width]
    arrive(got_vec)
    vec = total([vec_y[s] for s in range(SIDE)])
    second_gain_grad[...] = vec[0:1]
    conv_grad[...] = vec[1:4]
    first_gain_grad[...] = vec[4:5]

    mirrored = (swap_out, swap_down, back_down, back_out)

    @pl.when(x != z)
    def _():
        arrive((back_down, back_out))
        for c in mirrored:
            c.wait_send()

    for c in started:
        if not any(c is m for m in mirrored):
            c.wait_send()


def passing(*refs):
    n = len(refs) // 2
    sems = refs[-1]
    copies = [pltpu.make_async_copy(refs[i], refs[n + i], sems.at[i]) for i in range(n)]
    for c in copies:
        c.start()
    for c in copies:
        c.wait()


def body(
    tokens,
    run_counts,
    seq_lengths,
    first_gain,
    in_weight,
    conv_weight,
    out_weight,
    second_gain,
    gate_weight,
    up_weight,
    down_weight,
    cotangent,
):
    slots, width = tokens.shape
    wide = in_weight.shape[0]
    units, deep = gate_weight.shape[1], down_weight.shape[0]
    three = 3 * width
    features = SIDE * width

    def vm(*shape, dtype=bf16):
        return pltpu.VMEM(shape, dtype)

    gathered = [
        vm(SIDE, SIDE, 2, r, w)
        for r, w in ((wide, three), (wide, width), (wide, units), (wide, units), (deep, width))
    ]
    by_col = [vm(SIDE, slots, width) for _ in range(4)] + [vm(SIDE, 8, width, dtype=f32)]
    summed = [vm(SIDE, slots, width) for _ in range(8)] + [vm(SIDE, 8, slots, dtype=f32)]
    ones = [
        vm(SIDE, SIDE, r, w)
        for r, w in ((wide, three), (wide, width), (wide, units), (wide, units), (deep, width))
    ]
    twos = [
        vm(SIDE, SIDE, r, w)
        for r, w in (
            (wide, three // 2), (wide, three // 2), (wide, width),
            (wide, units), (wide, units), (deep, width // 2), (deep, width // 2),
        )
    ]
    threes = [
        vm(SIDE, r, w)
        for r, w in ((wide, three), (wide, width), (wide, units), (wide, units), (deep, width))
    ]
    turned = [vm(wide, width, dtype=f32), vm(deep, width, dtype=f32), vm(wide, width), vm(deep, width)]
    own = [
        vm(slots + 16, features), vm(slots, features), vm(SIDE, width, slots), vm(SIDE, width, slots),
        vm(slots, units), vm(units, slots), vm(slots, units), vm(slots, units),
        vm(slots, units, dtype=f32), vm(slots, three), vm(width, slots), vm(SIDE, slots, width),
    ]
    own += [vm(slots, width, dtype=f32) for _ in range(10)] + [vm(slots, 1, dtype=f32)]
    small = [vm(8, width, dtype=f32) for _ in range(5)] + [vm(SIDE, 8, width, dtype=f32) for _ in range(3)]
    scratch = gathered + by_col + summed + gathered + ones + twos + threes + turned + own + small
    scratch += [pltpu.SemaphoreType.DMA((COPIES,)), pltpu.SemaphoreType.DMA((COPIES,)), pltpu.SemaphoreType.DMA((9,))]

    vmem, smem = pl.BlockSpec(memory_space=pltpu.VMEM), pl.BlockSpec(memory_space=pltpu.SMEM)
    anywhere = pl.BlockSpec(memory_space=pltpu.HBM)

    def hbm(array):
        return pltpu.with_memory_space_constraint(array, pltpu.HBM)

    def out(*shape, dtype=f32):
        return jax.ShapeDtypeStruct(shape, dtype)

    shapes = (
        out(slots, width, dtype=bf16), out(slots, width), out(1, width), out(3, wide, width), out(3, width),
        out(wide, width), out(1, width), out(wide, units), out(wide, units), out(deep, width),
    )
    results = (
        pl.pallas_call(
            kernel,
            out_shape=tuple(pltpu.VMEM(a.shape, a.dtype) for a in shapes),
            in_specs=[anywhere, smem, smem, vmem, anywhere, vmem, anywhere, vmem] + [anywhere] * 4,
            out_specs=(vmem,) * 10,
            scratch_shapes=scratch,
            compiler_params=pltpu.CompilerParams(
                collective_id=0, has_side_effects=True, vmem_limit_bytes=60 * 2**20
            ),
            name="block",
        )(
            hbm(tokens), run_counts, seq_lengths, first_gain, hbm(in_weight.transpose(1, 0, 2)), conv_weight,
            hbm(out_weight), second_gain, hbm(gate_weight), hbm(up_weight), hbm(down_weight), hbm(cotangent),
        )
    )
    results = pl.pallas_call(
        passing,
        out_shape=shapes,
        in_specs=[vmem] * 10,
        out_specs=(anywhere,) * 10,
        scratch_shapes=[pltpu.SemaphoreType.DMA((10,))],
        name="results",
    )(*(pltpu.with_memory_space_constraint(r, pltpu.VMEM) for r in results))
    block_out, input_grad, first_grad, in_grad, conv_grad, out_grad, second_grad, gate_grad, up_grad, down_grad = results
    return (
        block_out,
        input_grad,
        first_grad.reshape(width),
        in_grad.transpose(1, 0, 2),
        conv_grad,
        out_grad,
        second_grad.reshape(width),
        gate_grad,
        up_grad,
        down_grad,
    )


def solution(mesh):
    return jax.shard_map(
        body,
        mesh=mesh,
        in_specs=(
            P("row", "col"),
            P(),
            P(),
            P("col"),
            P("row", None, "col"),
            P(None, "col"),
            P("row", "col"),
            P("col"),
            P("row", "col"),
            P("row", "col"),
            P("row", "col"),
            P("row", "col"),
        ),
        out_specs=(
            P("row", "col"),
            P("row", "col"),
            P("col"),
            P("row", None, "col"),
            P(None, "col"),
            P("row", "col"),
            P("col"),
            P("row", "col"),
            P("row", "col"),
            P("row", "col"),
        ),
        check_vma=False,
    )
```

```python
import functools

import jax
import jax.numpy as jnp
from jax import lax
from jax.experimental import pallas as pl
from jax.experimental.pallas import tpu as pltpu
from jax.sharding import PartitionSpec as P

epsilon = 1e-05
MESH = pl.DeviceIdType.MESH
bf16, f32 = jnp.bfloat16, jnp.float32
SIDE = 4
RING = (1, 3, 2)
COPIES = 256


def dot(a, b):
    return lax.dot_general(a, b, (((1,), (0,)), ((), ())), preferred_element_type=f32)


def dot_nt(a, b):
    return lax.dot_general(a, b, (((1,), (1,)), ((), ())), preferred_element_type=f32)


def wrap(i):
    return lax.rem(i, SIDE)


def total(values):
    return functools.reduce(lambda a, b: a + b, values)


def kernel(
    tokens, run_counts, seq_lengths, first_gain, in_weight, conv_weight, out_weight, second_gain,
    gate_weight, up_weight, down_weight, cotangent,
    block_out, input_grad, first_gain_grad, in_grad, conv_grad, out_grad, second_gain_grad,
    gate_grad, up_grad, down_grad,
    in_b, out_b, gate_b, up_b, down_b,
    x_g, cot_g, r1_g, gh2_g, gains,
    o_s, o_r, gh2_s, gh2_r, ffo_s, ffo_r, gh1_s, gh1_r, dots,
    in_p, out_p, gate_p, up_p, down_p,
    in_1, out_1, gate_1, up_1, down_1,
    in_2a, in_2b, out_2, gate_2, up_2, down_2a, down_2b,
    gate_v, up_v, down_va, down_vb,
    in_3, out_3, gate_3, up_3, down_3,
    out_t, down_t, out_i, down_i,
    h1, h2, h1_t, h2_t, hid, hid_t, g_gate_ref, g_up, g_hid, g_proj, z_t, go,
    b_s, c_s, x_s, conv_s, tap1_s, tap2_s, r1_s, gr1_s, own_s, ffo_own, rs1_s,
    tail_s, back_s, back_r, vec_a, vec_b, vec_x, vec_y, tail_g,
    send, recv, brought,
):
    row, z = lax.axis_index("row"), lax.axis_index("col")
    x, y, k = row // (2 * SIDE), wrap(row // 2), lax.rem(row, 2)
    slots, width = tokens.shape
    rows = 2 * SIDE * SIDE

    def at(x_to, y_to, k_to, z_to):
        return ((wrap(x_to) * SIDE + wrap(y_to)) * 2 + k_to, wrap(z_to))

    def x_peer(d):
        return at(x + d, y, k, z)

    def y_peer(d):
        return at(x, y + d, k, z)

    def z_peer(d):
        return (row, wrap(z + d))

    sibling = (row + 1 - 2 * k, z)
    mirror = at(z, y, k, x)
    next_row, last_row = (lax.rem(row + 1, rows), z), (lax.rem(row + rows - 1, rows), z)

    local = []

    def bring(src, dst):
        c = pltpu.make_async_copy(src, dst, brought.at[len(local)])
        local.append(c)
        c.start()

    for p in range(3):
        bring(in_weight.at[p], in_b.at[x, y, k, :, p * width : (p + 1) * width])
    bring(tokens, x_g.at[z])
    bring(gate_weight, gate_b.at[x, y, k])
    bring(up_weight, up_b.at[x, y, k])
    bring(cotangent, cot_g.at[z])
    bring(out_weight, out_i)
    bring(down_weight, down_i)
    barrier = pltpu.get_barrier_semaphore()
    peers = [f(d) for f in (x_peer, y_peer, z_peer) for d in RING] + [next_row, last_row]
    for peer in peers:
        pl.semaphore_signal(barrier, inc=1, device_id=peer, device_id_type=MESH)

    @pl.when(x != z)
    def _():
        pl.semaphore_signal(barrier, inc=1, device_id=mirror, device_id_type=MESH)

    gains[z, 0:1, :] = first_gain[...].astype(f32).reshape(1, width)
    gains[z, 1:2, :] = second_gain[...].astype(f32).reshape(1, width)
    gains[z, 2:8, :] = jnp.zeros((6, width), f32)
    for c in local:
        c.wait()

    @pl.when(x != z)
    def _():
        pl.semaphore_wait(barrier, len(peers) + 1)

    @pl.when(x == z)
    def _():
        pl.semaphore_wait(barrier, len(peers))

    started = []

    def copy(src, dst, to):
        i = len(started)
        c = pltpu.make_async_remote_copy(
            src_ref=src,
            dst_ref=dst,
            send_sem=send.at[i],
            recv_sem=recv.at[i],
            device_id=to,
            device_id_type=MESH,
        )
        started.append(c)
        return c

    def launch(src, dst, to):
        c = copy(src, dst, to)
        c.start()
        return c

    def arrive(copies):
        for c in copies:
            c.wait_recv()

    def gather_z(buf):
        return [launch(buf.at[z], buf.at[z], z_peer(d)) for d in RING]

    class Gather:
        def __init__(self, buf, first, cols=None, relayed=False):
            self.buf, self.first, self.relayed = buf, first, relayed
            self.cols = slice(None) if cols is None else pl.ds(*cols)

        def ring_one(self):
            own = self.buf.at[x, y, k, :, self.cols]
            peer = x_peer if self.first == "x" else y_peer
            self.pending = [launch(own, own, peer(d)) for d in RING]

        def ring_two(self):
            arrive(self.pending)
            if self.first == "x":
                part, peer = self.buf.at[:, y, k, :, self.cols], y_peer
            else:
                part, peer = self.buf.at[x, :, k, :, self.cols], x_peer
            self.pending = [launch(part, part, peer(d)) for d in (RING[:2] if self.relayed else RING)]

        def relay(self):
            arrive(self.pending)
            low, high = slice(0, SIDE // 2), slice(SIDE // 2, SIDE)
            if self.first == "x":
                up, down = self.buf.at[low, wrap(y + 3), k, :, self.cols], self.buf.at[high, wrap(y + 1), k, :, self.cols]
                peer = y_peer
            else:
                up, down = self.buf.at[wrap(x + 3), low, k, :, self.cols], self.buf.at[wrap(x + 1), high, k, :, self.cols]
                peer = x_peer
            self.pending = [launch(up, up, peer(1)), launch(down, down, peer(3))]

        def core(self):
            arrive(self.pending)
            part = self.buf.at[:, :, k, :, self.cols]
            self.pending = [launch(part, part, sibling)]

        def done(self):
            arrive(self.pending)

    class Scatter:
        def __init__(self, partial, one, parts, three):
            self.partial, self.one, self.parts, self.three = partial, one, parts, three

        def core(self):
            self.pending = [launch(self.partial.at[:, :, 1 - k], self.one, sibling)]

        def ring_one(self):
            arrive(self.pending)
            one, partial = self.one, self.partial

            @pl.loop(0, SIDE * SIDE)
            def _(i):
                a, b = i // SIDE, wrap(i)
                one[a, b] = (partial[a, b, k].astype(f32) + one[a, b].astype(f32)).astype(bf16)

            self.pending = []
            for two, first, cols in self.parts:
                cs = pl.ds(*cols)
                sent = []
                for d in RING:
                    if first == "x":
                        part, peer, me = one.at[wrap(x + d), :, :, cs], x_peer(d), x
                    else:
                        part, peer, me = one.at[:, wrap(y + d), :, cs], y_peer(d), y
                    sent.append(launch(part, two.at[me], peer))
                self.pending.append(sent)
                if first == "x":
                    two[x] = one[x, :, :, cs]
                else:
                    two[y] = one[:, y, :, cs]

        def ring_two(self):
            later = []
            for (two, first, cols), sent in zip(self.parts, self.pending):
                arrive(sent)
                me = x if first == "x" else y

                @pl.loop(0, SIDE)
                def _(j):
                    two[me, j] = total([two[s, j].astype(f32) for s in range(SIDE)]).astype(bf16)

                cs = pl.ds(*cols)
                for d in RING:
                    if first == "x":
                        part, peer, to = two.at[x, wrap(y + d)], y_peer(d), y
                    else:
                        part, peer, to = two.at[y, wrap(x + d)], x_peer(d), x
                    later.append(launch(part, self.three.at[to, :, cs], peer))
                if first == "x":
                    self.three[y, :, cs] = two[x, y]
                else:
                    self.three[x, :, cs] = two[y, x]
            self.pending = later

        def done(self):
            arrive(self.pending)
            return total([self.three[s].astype(f32) for s in range(SIDE)])

    class Relay(Scatter):
        def ring_one(self):
            arrive(self.pending)
            one, partial = self.one, self.partial

            @pl.loop(0, SIDE * SIDE)
            def _(i):
                a, b = i // SIDE, wrap(i)
                one[a, b] = (partial[a, b, k].astype(f32) + one[a, b].astype(f32)).astype(bf16)

            low, high = slice(0, SIDE // 2), slice(SIDE // 2, SIDE)
            self.pending = []
            for two, via, first, cols in self.parts:
                cs = pl.ds(*cols)
                if first == "x":
                    far = wrap(x + 2)
                    up, down, peer = one.at[far, low, :, cs], one.at[far, high, :, cs], x_peer
                else:
                    far = wrap(y + 2)
                    up, down, peer = one.at[low, far, :, cs], one.at[high, far, :, cs], y_peer
                self.pending.append([launch(up, via.at[0], peer(1)), launch(down, via.at[1], peer(3))])

        def relay(self):
            one, later = self.one, []
            for (two, via, first, cols), sent in zip(self.parts, self.pending):
                arrive(sent)
                cs = pl.ds(*cols)
                for j in range(SIDE // 2):
                    if first == "x":
                        a, b = (wrap(x + 1), j), (wrap(x + 3), j + SIDE // 2)
                    else:
                        a, b = (j, wrap(y + 1)), (j + SIDE // 2, wrap(y + 3))
                    for n, at_n in ((0, a), (1, b)):
                        both = one[at_n[0], at_n[1], :, cs].astype(f32) + via[n, j].astype(f32)
                        one[at_n[0], at_n[1], :, cs] = both.astype(bf16)
                if first == "x":
                    up, down, peer = one.at[wrap(x + 1), :, :, cs], one.at[wrap(x + 3), :, :, cs], x_peer
                else:
                    up, down, peer = one.at[:, wrap(y + 1), :, cs], one.at[:, wrap(y + 3), :, cs], y_peer
                later.append([launch(up, two.at[0], peer(1)), launch(down, two.at[1], peer(3))])
            self.pending = later

        def ring_two(self):
            one, later = self.one, []
            for (two, via, first, cols), sent in zip(self.parts, self.pending):
                arrive(sent)
                cs = pl.ds(*cols)
                for j in range(SIDE):
                    own = one[x, j, :, cs] if first == "x" else one[j, y, :, cs]
                    two[0, j] = (own.astype(f32) + two[0, j].astype(f32) + two[1, j].astype(f32)).astype(bf16)
                to = y if first == "x" else x
                peer = y_peer if first == "x" else x_peer
                for d in RING:
                    later.append(launch(two.at[0, wrap(to + d)], self.three.at[to, :, cs], peer(d)))
                self.three[to, :, cs] = two[0, to]
            self.pending = later

    in_half = in_b.shape[-1] // 2
    half = width // 2
    g_in = [Gather(in_b, "x", (0, in_half)), Gather(in_b, "y", (in_half, in_half))]
    g_out = Gather(out_b, "x")
    g_down = [Gather(down_b, "x", (0, half), True), Gather(down_b, "y", (half, half), True)]
    w_gate, w_up = Gather(gate_b, "x", None, True), Gather(up_b, "y", None, True)
    for g in g_in:
        g.ring_one()
    got_x = gather_z(x_g) + gather_z(gains)

    slot = lax.broadcasted_iota(jnp.int32, (slots, 1), 0)
    count = run_counts[row]
    offset = total([jnp.where(q < row, run_counts[q], 0) for q in range(rows)])
    position = offset + slot
    is_live = slot < count
    start, seq_start = 0, jnp.zeros((slots, 1), jnp.int32)
    for q in range(seq_lengths.shape[0]):
        seq_start = jnp.maximum(seq_start, jnp.where(position >= start, start, 0))
        start = start + seq_lengths[q]
    valid1 = is_live & (position - 1 >= seq_start)
    valid2 = is_live & (position - 2 >= seq_start)


    def last_two(values):
        one = jnp.sum(jnp.where(slot == count - 2, values, 0.0), axis=0, keepdims=True)
        two = jnp.sum(jnp.where(slot == count - 1, values, 0.0), axis=0, keepdims=True)
        return one, two

    tail_s[...] = jnp.zeros(tail_s.shape, f32)
    tail_s[0:1, :], tail_s[1:2, :] = last_two(x_g[z].astype(f32))
    got_tail = launch(tail_s, tail_g.at[z], next_row)
    swap_out = copy(out_i, out_b.at[z, y, k], mirror)
    swap_down = copy(down_i, down_b.at[z, y, k], mirror)

    @pl.when(x != z)
    def _():
        swap_out.start()
        swap_down.start()

    @pl.when(x == z)
    def _():
        out_b[x, y, k] = out_i[...]
        down_b[x, y, k] = down_i[...]

    for g in g_in:
        g.ring_two()
    got_tail.wait_recv()
    got_tail = gather_z(tail_g)

    @pl.when(x != z)
    def _():
        swap_out.wait_recv()
        swap_down.wait_recv()

    g_out.ring_one()
    w_gate.ring_one()
    w_up.ring_one()
    for g in g_down:
        g.ring_one()
    cot_g[z] = jnp.where(is_live, cot_g[z].astype(f32), 0.0).astype(bf16)
    got_cot = gather_z(cot_g)

    arrive(got_x)
    g_out.ring_two()
    w_gate.ring_two()
    w_up.ring_two()
    for g in g_down:
        g.ring_two()
    features = SIDE * width

    def scale(values):
        return lax.rsqrt(total([jnp.sum(jnp.square(v), axis=1, keepdims=True) for v in values]) / features + epsilon)

    rs1_s[...] = scale([x_g[i].astype(f32) for i in range(SIDE)])
    for i in range(SIDE):
        h = ((x_g[i].astype(f32) * rs1_s[...]) * gains[i, 0:1, :]).astype(bf16)
        h1[0:slots, i * width : (i + 1) * width] = h
    for g in g_in:
        g.core()
    arrive(got_tail)
    tail_scale = scale([tail_g[i] for i in range(SIDE)])
    for i in range(SIDE):
        h = (tail_g[i] * tail_scale) * gains[i, 0:1, :]
        h = jnp.concatenate([h, jnp.zeros(h.shape, f32)], axis=0).astype(bf16)
        h1[slots : slots + 16, i * width : (i + 1) * width] = h
    for i in range(SIDE):
        h1_t[i] = h1[0:slots, i * width : (i + 1) * width].T

    for g in g_in:
        g.done()

    def in_part(p, tokens_of):
        return dot(tokens_of, in_b[:, :, :, :, p * width : (p + 1) * width].reshape(features, width))

    b_all, x_all = in_part(0, h1[...]), in_part(2, h1[...])
    b_s[...], x_s[...] = b_all[0:slots], x_all[0:slots]
    c_s[...] = in_part(1, h1[0:slots, :])
    u_all = (b_all * x_all).astype(bf16).astype(f32)
    u, halo = u_all[0:slots], u_all[slots : slots + 8]
    g_out.core()
    taps = conv_weight[...].astype(f32)
    tap1 = pltpu.roll(u, 1, 0)
    tap2 = pltpu.roll(u, 2, 0)
    tap1 = jnp.where(valid1, jnp.where(slot == 0, halo[1:2], tap1), 0.0)
    tap2 = jnp.where(valid2, jnp.where(slot == 0, halo[0:1], jnp.where(slot == 1, halo[1:2], tap2)), 0.0)
    tap1_s[...] = tap1
    tap2_s[...] = tap2
    conv = taps[0:1] * u + taps[1:2] * tap1 + taps[2:3] * tap2
    conv_s[...] = conv
    mixed = (c_s[...] * conv).astype(bf16)
    z_t[...] = mixed.T
    g_out.done()

    got_o = []
    for d in RING:
        i = wrap(z + d)
        o_s[i] = dot(mixed, out_b[i].reshape(width, width)).astype(bf16)
        got_o.append(launch(o_s.at[i], o_r.at[z], z_peer(d)))
    r1_s[...] = x_g[z].astype(f32) + dot(mixed, out_b[z].reshape(width, width))
    arrive(got_o)
    r1 = r1_s[...] + total([o_r[wrap(z + d)].astype(f32) for d in RING])
    r1_s[...] = r1
    r1_g[z] = r1.astype(bf16)
    got_r1 = gather_z(r1_g)
    w_gate.relay()
    w_up.relay()
    for g in g_down:
        g.relay()

    arrive(got_cot)
    w_gate.core()
    w_up.core()
    for g in g_down:
        g.core()
    units = hid.shape[1]

    arrive(got_r1)
    rs2 = scale([r1_g[i].astype(f32) for i in range(SIDE)])
    for i in range(SIDE):
        h = ((r1_g[i].astype(f32) * rs2) * gains[i, 1:2, :]).astype(bf16)
        h2[:, i * width : (i + 1) * width] = h

    w_gate.done()
    w_up.done()
    for g in g_down:
        g.done()
    g_hid[...] = total([dot_nt(cot_g[i], down_b[i].reshape(units, width)) for i in range(SIDE)])
    tile = units // 3
    for n in range(3):
        cs = slice(n * tile, (n + 1) * tile)
        gate = dot(h2[...], gate_b[:, :, :, :, cs].reshape(features, tile))
        up = dot(h2[...], up_b[:, :, :, :, cs].reshape(features, tile))
        sigma = jax.nn.sigmoid(gate)
        swish = gate * sigma
        grad = g_hid[:, cs]
        hid[:, cs] = (swish * up).astype(bf16)
        g_gate_n = grad * up * sigma * (1.0 + gate * (1.0 - sigma))
        g_gate_ref[:, cs] = g_gate_n.astype(bf16)
        g_up[:, cs] = (grad * swish).astype(bf16)

    def h2_part(i):
        return dot_nt(g_gate_ref[...], gate_b[i].reshape(width, units)) + dot_nt(
            g_up[...], up_b[i].reshape(width, units)
        )

    got_gh2 = []
    for d in RING:
        i = wrap(z + d)
        gh2_s[i] = h2_part(i).astype(bf16)
        got_gh2.append(launch(gh2_s.at[i], gh2_r.at[z], z_peer(d)))
    own_s[...] = h2_part(z)
    hid_t[...] = hid[...].T

    @pl.loop(0, SIDE)
    def _(i):
        down_p[i] = dot(hid_t[...], cot_g[i]).astype(bf16).reshape(down_p.shape[1:])

    s_down = Relay(down_p, down_1, [(down_2a, down_va, "x", (0, half)), (down_2b, down_vb, "y", (half, half))], down_3)
    s_down.core()
    for i in range(SIDE):
        h2_t[i] = h2[:, i * width : (i + 1) * width].T

    @pl.loop(0, SIDE)
    def _(i):
        gate_p[i] = dot(h2_t[i], g_gate_ref[...]).astype(bf16).reshape(gate_p.shape[1:])

    s_gate = Relay(gate_p, gate_1, [(gate_2, gate_v, "x", (0, units))], gate_3)
    s_gate.core()
    arrive(got_gh2)
    gh2_g[z] = (own_s[...] + total([gh2_r[wrap(z + d)].astype(f32) for d in RING])).astype(bf16)
    got_gh2 = gather_z(gh2_g)
    s_down.ring_one()

    @pl.loop(0, SIDE)
    def _(i):
        up_p[i] = dot(h2_t[i], g_up[...]).astype(bf16).reshape(up_p.shape[1:])

    s_up = Relay(up_p, up_1, [(up_2, up_v, "y", (0, units))], up_3)
    s_up.core()
    s_gate.ring_one()
    s_up.ring_one()
    s_down.relay()

    for d in RING:
        i = wrap(z + d)
        ffo_s[i] = dot(hid[...], down_b[i].reshape(units, width)).astype(bf16)
    ffo_own[...] = r1_s[...] + dot(hid[...], down_b[z].reshape(units, width))

    arrive(got_gh2)
    got_ffo = [launch(ffo_s.at[wrap(z + d)], ffo_r.at[z], z_peer(d)) for d in RING]
    mean2 = total(
        [
            jnp.sum(gh2_g[i].astype(f32) * gains[i, 1:2, :] * (r1_g[i].astype(f32) * rs2), axis=1, keepdims=True)
            for i in range(SIDE)
        ]
    ) / features

    def r1_grad(i):
        n2 = r1_g[i].astype(f32) * rs2
        return cot_g[i].astype(f32) + rs2 * (gh2_g[i].astype(f32) * gains[i, 1:2, :] - n2 * mean2)

    for i in range(SIDE):
        go[i] = r1_grad(i).astype(bf16)
    gr1_s[...] = r1_grad(z)
    vec_a[...] = jnp.zeros(vec_a.shape, f32)
    vec_a[0:1, :] = jnp.sum(gh2_g[z].astype(f32) * (r1_g[z].astype(f32) * rs2), axis=0, keepdims=True)

    g_z = total([dot_nt(go[i], out_b[i].reshape(width, width)) for i in range(SIDE)])
    g_c = g_z * conv_s[...]
    g_v = g_z * c_s[...]
    u = (b_s[...] * x_s[...]).astype(bf16).astype(f32)
    into1 = jnp.where(valid1, taps[1:2] * g_v, 0.0)
    into2 = jnp.where(valid2, taps[2:3] * g_v, 0.0)
    back_s[...] = jnp.zeros(back_s.shape, f32)
    back_s[0:1, :] = into2[0:1, :]
    back_s[1:2, :] = into1[0:1, :] + into2[1:2, :]
    got_back = launch(back_s, back_r, last_row)
    for i in range(SIDE):
        out_p[i] = dot(z_t[...], go[i]).astype(bf16).reshape(out_p.shape[1:])
    s_out = Scatter(out_p, out_1, [(out_2, "y", (0, width))], out_3)
    s_out.core()
    vec_a[1:2, :] = jnp.sum(g_v * u, axis=0, keepdims=True)
    vec_a[2:3, :] = jnp.sum(g_v * tap1_s[...], axis=0, keepdims=True)
    vec_a[3:4, :] = jnp.sum(g_v * tap2_s[...], axis=0, keepdims=True)
    g_u = taps[0:1] * g_v
    g_u = g_u + jnp.where(slot < slots - 1, pltpu.roll(into1, slots - 1, 0), 0.0)
    g_u = g_u + jnp.where(slot < slots - 2, pltpu.roll(into2, slots - 2, 0), 0.0)
    got_back.wait_recv()
    back = back_r[...]
    g_u = g_u + jnp.where(slot == count - 2, back[0:1], 0.0) + jnp.where(slot == count - 1, back[1:2], 0.0)
    g_proj[:, 0:width] = (g_u * x_s[...]).astype(bf16)
    g_proj[:, width : 2 * width] = g_c.astype(bf16)
    g_proj[:, 2 * width : 3 * width] = (g_u * b_s[...]).astype(bf16)

    for i in range(SIDE):
        in_p[i] = dot(h1_t[i], g_proj[...]).astype(bf16).reshape(in_p.shape[1:])
    s_in = Scatter(in_p, in_1, [(in_2a, "x", (0, in_half)), (in_2b, "y", (in_half, in_half))], in_3)
    s_in.core()
    s_gate.relay()
    s_up.relay()

    ones = jnp.ones((8, width), bf16)

    def h1_part(i):
        part = dot_nt(g_proj[...], in_b[i].reshape(width, 3 * width))
        n1 = x_g[i].astype(f32) * rs1_s[...]
        return part, dot_nt(ones, (part * gains[i, 0:1, :] * n1).astype(bf16))

    got_gh1, along = [], []
    for d in RING:
        i = wrap(z + d)
        part, one = h1_part(i)
        along.append(one)
        gh1_s[i] = part.astype(bf16)
        got_gh1.append(launch(gh1_s.at[i], gh1_r.at[z], z_peer(d)))
    part, one = h1_part(z)
    own_s[...] = part
    dots[z] = total(along) + one
    got_gh1 += gather_z(dots)
    s_in.ring_one()
    s_out.ring_one()
    s_down.ring_two()

    s_gate.ring_two()
    s_up.ring_two()

    arrive(got_gh1)
    gh1 = own_s[...] + total([gh1_r[wrap(z + d)].astype(f32) for d in RING])
    mean1 = total([dots[i] for i in range(SIDE)]).T[:, 0:1] / features
    n1 = x_g[z].astype(f32) * rs1_s[...]
    input_grad[...] = gr1_s[...] + rs1_s[...] * (gh1 * gains[z, 0:1, :] - n1 * mean1)
    vec_a[4:5, :] = jnp.sum(gh1 * n1, axis=0, keepdims=True)
    got_vec = launch(vec_a, vec_b, sibling)

    down_t[...] = s_down.done()
    back_down = copy(down_t, down_grad, mirror)

    @pl.when(x != z)
    def _():
        back_down.start()

    @pl.when(x == z)
    def _():
        down_grad[...] = down_t[...]

    s_in.ring_two()
    s_out.ring_two()
    got_vec.wait_recv()
    vec_x[x] = vec_a[...] + vec_b[...]
    got_vec = [launch(vec_x.at[x], vec_x.at[x], x_peer(d)) for d in RING]
    gate_grad[...] = s_gate.done()
    up_grad[...] = s_up.done()
    arrive(got_vec)
    vec_y[y] = total([vec_x[s] for s in range(SIDE)])
    got_vec = [launch(vec_y.at[y], vec_y.at[y], y_peer(d)) for d in RING]
    out_t[...] = s_out.done()
    back_out = copy(out_t, out_grad, mirror)

    @pl.when(x != z)
    def _():
        back_out.start()

    @pl.when(x == z)
    def _():
        out_grad[...] = out_t[...]

    arrive(got_ffo)
    ffo = ffo_own[...] + total([ffo_r[wrap(z + d)].astype(f32) for d in RING])
    block_out[...] = jnp.where(is_live, ffo, 0.0).astype(bf16)
    in_sum = s_in.done()
    for p in range(3):
        in_grad[p] = in_sum[:, p * width : (p + 1) * width]
    arrive(got_vec)
    vec = total([vec_y[s] for s in range(SIDE)])
    second_gain_grad[...] = vec[0:1]
    conv_grad[...] = vec[1:4]
    first_gain_grad[...] = vec[4:5]

    mirrored = (swap_out, swap_down, back_down, back_out)

    @pl.when(x != z)
    def _():
        arrive((back_down, back_out))
        for c in mirrored:
            c.wait_send()

    for c in started:
        if not any(c is m for m in mirrored):
            c.wait_send()


def passing(*refs):
    n = len(refs) // 2
    sems = refs[-1]
    copies = [pltpu.make_async_copy(refs[i], refs[n + i], sems.at[i]) for i in range(n)]
    for c in copies:
        c.start()
    for c in copies:
        c.wait()


def body(
    tokens,
    run_counts,
    seq_lengths,
    first_gain,
    in_weight,
    conv_weight,
    out_weight,
    second_gain,
    gate_weight,
    up_weight,
    down_weight,
    cotangent,
):
    slots, width = tokens.shape
    wide = in_weight.shape[0]
    units, deep = gate_weight.shape[1], down_weight.shape[0]
    three = 3 * width
    features = SIDE * width

    def vm(*shape, dtype=bf16):
        return pltpu.VMEM(shape, dtype)

    gathered = [
        vm(SIDE, SIDE, 2, r, w)
        for r, w in ((wide, three), (wide, width), (wide, units), (wide, units), (deep, width))
    ]
    by_col = [vm(SIDE, slots, width) for _ in range(4)] + [vm(SIDE, 8, width, dtype=f32)]
    summed = [vm(SIDE, slots, width) for _ in range(8)] + [vm(SIDE, 8, slots, dtype=f32)]
    ones = [
        vm(SIDE, SIDE, r, w)
        for r, w in ((wide, three), (wide, width), (wide, units), (wide, units), (deep, width))
    ]
    twos = [vm(SIDE, SIDE, wide, w) for w in (three // 2, three // 2, width)]
    relayed = ((wide, units), (wide, units), (deep, width // 2), (deep, width // 2))
    twos += [vm(2, SIDE, r, w) for r, w in relayed] + [vm(2, SIDE // 2, r, w) for r, w in relayed]
    threes = [
        vm(SIDE, r, w)
        for r, w in ((wide, three), (wide, width), (wide, units), (wide, units), (deep, width))
    ]
    turned = [vm(wide, width, dtype=f32), vm(deep, width, dtype=f32), vm(wide, width), vm(deep, width)]
    own = [
        vm(slots + 16, features), vm(slots, features), vm(SIDE, width, slots), vm(SIDE, width, slots),
        vm(slots, units), vm(units, slots), vm(slots, units), vm(slots, units),
        vm(slots, units, dtype=f32), vm(slots, three), vm(width, slots), vm(SIDE, slots, width),
    ]
    own += [vm(slots, width, dtype=f32) for _ in range(10)] + [vm(slots, 1, dtype=f32)]
    small = [vm(8, width, dtype=f32) for _ in range(5)] + [vm(SIDE, 8, width, dtype=f32) for _ in range(3)]
    scratch = gathered + by_col + summed + gathered + ones + twos + threes + turned + own + small
    scratch += [pltpu.SemaphoreType.DMA((COPIES,)), pltpu.SemaphoreType.DMA((COPIES,)), pltpu.SemaphoreType.DMA((9,))]

    vmem, smem = pl.BlockSpec(memory_space=pltpu.VMEM), pl.BlockSpec(memory_space=pltpu.SMEM)
    anywhere = pl.BlockSpec(memory_space=pltpu.HBM)

    def hbm(array):
        return pltpu.with_memory_space_constraint(array, pltpu.HBM)

    def out(*shape, dtype=f32):
        return jax.ShapeDtypeStruct(shape, dtype)

    shapes = (
        out(slots, width, dtype=bf16), out(slots, width), out(1, width), out(3, wide, width), out(3, width),
        out(wide, width), out(1, width), out(wide, units), out(wide, units), out(deep, width),
    )
    results = (
        pl.pallas_call(
            kernel,
            out_shape=tuple(pltpu.VMEM(a.shape, a.dtype) for a in shapes),
            in_specs=[anywhere, smem, smem, vmem, anywhere, vmem, anywhere, vmem] + [anywhere] * 4,
            out_specs=(vmem,) * 10,
            scratch_shapes=scratch,
            compiler_params=pltpu.CompilerParams(
                collective_id=0, has_side_effects=True, vmem_limit_bytes=60 * 2**20
            ),
            name="block",
        )(
            hbm(tokens), run_counts, seq_lengths, first_gain, hbm(in_weight.transpose(1, 0, 2)), conv_weight,
            hbm(out_weight), second_gain, hbm(gate_weight), hbm(up_weight), hbm(down_weight), hbm(cotangent),
        )
    )
    results = pl.pallas_call(
        passing,
        out_shape=shapes,
        in_specs=[vmem] * 10,
        out_specs=(anywhere,) * 10,
        scratch_shapes=[pltpu.SemaphoreType.DMA((10,))],
        name="results",
    )(*(pltpu.with_memory_space_constraint(r, pltpu.VMEM) for r in results))
    block_out, input_grad, first_grad, in_grad, conv_grad, out_grad, second_grad, gate_grad, up_grad, down_grad = results
    return (
        block_out,
        input_grad,
        first_grad.reshape(width),
        in_grad.transpose(1, 0, 2),
        conv_grad,
        out_grad,
        second_grad.reshape(width),
        gate_grad,
        up_grad,
        down_grad,
    )


def solution(mesh):
    return jax.shard_map(
        body,
        mesh=mesh,
        in_specs=(
            P("row", "col"),
            P(),
            P(),
            P("col"),
            P("row", None, "col"),
            P(None, "col"),
            P("row", "col"),
            P("col"),
            P("row", "col"),
            P("row", "col"),
            P("row", "col"),
            P("row", "col"),
        ),
        out_specs=(
            P("row", "col"),
            P("row", "col"),
            P("col"),
            P("row", None, "col"),
            P(None, "col"),
            P("row", "col"),
            P("col"),
            P("row", "col"),
            P("row", "col"),
            P("row", "col"),
        ),
        check_vma=False,
    )
```
